32 devices in a mesh: grp: 2 (over y), gx: 8 (over z, x), gy: 2 (over core).
Axes of the slice: x: 2, y: 2, z: 4, core: 2. Of those that a mesh axis runs over, the one named last changes fastest.
Arguments:
- activations: bfloat16 [256, 8192], P('grp', 'gx'), parts along dimension 0, may hold values from -6 to 6
- upstream: bfloat16 [256, 8192], P('grp', 'gx'), parts along dimension 0, may hold values from -6 to 6
- head_grad: bfloat16 [256, 8192], P('grp', 'gx'), parts along dimension 0, may hold values from -6 to 6
- target_mask: int32 [256], P('grp'), parts along dimension 0, may hold values 0 or 1
- gate_weight: bfloat16 [8192, 26624], P('gx', 'gy'), may hold values from -0.09375 to 0.09375
- up_weight: bfloat16 [8192, 26624], P('gx', 'gy'), may hold values from -0.09375 to 0.09375
- down_weight: bfloat16 [26624, 8192], P('gy', 'gx'), may hold values from -0.0546875 to 0.0546875
Outputs:
- input_grad: bfloat16 [256, 8192], P('grp', 'gx'), parts along dimension 0
The draws below stay inside these ranges and needn't reach their ends.
There are 2 independent parts, one for each index of `grp`. The reference program is written for one: setup_inputs(seed, part) draws one part's arguments, and reference() takes and returns one part's arrays. A program takes and returns all parts, laid end to end along the dimension named above; an argument that names none is the same for every part. Nothing has to cross between parts.
All inputs are finite; a program needn't handle non-finite values.
Results may differ from the reference program's by a relative error of at most 0.0055.
Values may be sent and summed in bfloat16 or wider, within the bound.
A program may use at most 448 MiB of HBM per device.

```python
import jax
import jax.numpy as jnp
from jax import lax

D = 8192
FF = 26624
ROWS = 128


def touch_ends(drawn, key, low, high):
    extent = drawn.shape
    spot = [jax.random.randint(jax.random.fold_in(key, axis), (), 0, extent[axis]) for axis in range(len(extent))]
    drawn = drawn.at[tuple(spot)].set(low)
    longest = extent.index(max(extent))
    spot[longest] = (spot[longest] + 1) % extent[longest]
    return drawn.at[tuple(spot)].set(high)


def strengthened(entries, stream_key, source, target, shards_of, factor):
    owner, partner = [(jnp.arange(entries.shape[position]) // (entries.shape[position] // shards_of)).reshape([-1 if axis == position else 1 for axis in range(entries.ndim)]) for position in (source, target)]
    chosen = jax.random.permutation(stream_key, shards_of)[partner]
    strong = (owner == chosen) | (owner == (partner + shards_of // 2) % shards_of)
    return jnp.where(strong, factor * entries, entries)


def level_of(own_key, dims, split, low, high):
    def one(axis_at, blocks):
        steps = jax.random.uniform(jax.random.fold_in(jax.random.fold_in(own_key, 6), axis_at), (blocks,), jnp.float32, low / len(split), high / len(split))
        return jnp.repeat(jnp.exp(steps), dims[axis_at] // blocks).reshape((-1,) + (1,) * (len(dims) - axis_at - 1))

    gain = one(*split[0])
    for cut in split[1:]:
        gain = gain * one(*cut)
    return gain


def gaussian(key, extent, scale, reach, pieces=(), kind=jnp.bfloat16):
    gain = level_of(key, extent, pieces, -0.22, 0.18) if pieces else 1.0
    array = jax.random.normal(key, extent, jnp.float32) * scale * gain
    return jnp.minimum(jnp.maximum(array, -reach), reach).astype(kind)


def bell_draw_with(stream_key, extent, scale, limit, cuts, heavy, held_as=jnp.bfloat16):
    drawn = scale * jax.random.normal(stream_key, extent, jnp.float32)
    if cuts:
        drawn = drawn * level_of(stream_key, extent, cuts, -0.22, 0.18)
    return jnp.clip(strengthened(drawn, jax.random.fold_in(stream_key, 3), *heavy), -limit, limit).astype(held_as)


def setup_inputs(seed: int = 0, part: int = 0) -> dict:
    keys = jax.random.split(jax.random.key(seed), 8)
    own_keys = jax.random.split(jax.random.fold_in(keys[7], part), 8)
    return {
        "activations": gaussian(own_keys[0], (ROWS, D), 1.0, 6.0, ((1, 8),)),
        "upstream": gaussian(own_keys[1], (ROWS, D), 1.0, 6.0, ((1, 8),)),
        "head_grad": gaussian(own_keys[2], (ROWS, D), 1.0, 6.0, ((1, 8),)),
        "target_mask": touch_ends((jax.random.randint(own_keys[3], (ROWS,), 0, 3) < 1).astype(jnp.int32), jax.random.fold_in(own_keys[3], 1), 0, 1),
        "gate_weight": bell_draw_with(keys[4], (D, FF), D ** -0.5, 0.09375, ((0, 8), (1, 2)), (1, 0, 8, 2.0)),
        "up_weight": bell_draw_with(keys[5], (D, FF), D ** -0.5, 0.09375, ((0, 8), (1, 2)), (1, 0, 8, 2.0)),
        "down_weight": bell_draw_with(keys[6], (FF, D), FF ** -0.5, 0.0546875, ((0, 2), (1, 8)), (0, 1, 8, 2.0)),
    }


def transposed(left, weight):
    return lax.dot_general(left, weight, (((1,), (1,)), ((), ())), preferred_element_type=jnp.float32)


def swiglu_grads(gate_proj, up_proj, hidden_grad):
    sigmoid_gate = jax.nn.sigmoid(gate_proj)
    gate_grad = hidden_grad * up_proj * sigmoid_gate * (1.0 + gate_proj * (1.0 - sigmoid_gate))
    up_grad = hidden_grad * gate_proj * sigmoid_gate
    return gate_grad.astype(jnp.bfloat16), up_grad.astype(jnp.bfloat16)


def reference(activations, upstream, head_grad, target_mask, gate_weight, up_weight, down_weight):
    weights_mask = target_mask.astype(jnp.float32)[:, None]
    cotangent = (upstream.astype(jnp.float32) + weights_mask * head_grad.astype(jnp.float32)).astype(jnp.bfloat16)
    gate_proj = jnp.dot(activations, gate_weight, preferred_element_type=jnp.float32)
    up_proj = jnp.dot(activations, up_weight, preferred_element_type=jnp.float32)
    hidden_grad = transposed(cotangent, down_weight)
    gate_grad, up_grad = swiglu_grads(gate_proj, up_proj, hidden_grad)
    total_grad = transposed(gate_grad, gate_weight) + transposed(up_grad, up_weight)
    return total_grad.astype(jnp.bfloat16)
```

```python
import jax
import jax.numpy as jnp
from jax import lax
from jax.sharding import PartitionSpec as P


def transposed(left, weight):
    return lax.dot_general(
        left, weight, (((1,), (1,)), ((), ())), preferred_element_type=jnp.float32
    )


def swiglu_grads(gate_proj, up_proj, hidden_grad):
    sigmoid_gate = jax.nn.sigmoid(gate_proj)
    gate_grad = hidden_grad * up_proj * sigmoid_gate * (1.0 + gate_proj * (1.0 - sigmoid_gate))
    up_grad = hidden_grad * gate_proj * sigmoid_gate
    return (gate_grad.astype(jnp.bfloat16), up_grad.astype(jnp.bfloat16))


def shards(activations, upstream, head_grad, target_mask, gate_weight, up_weight, down_weight):
    rows = activations.shape[0]
    weights_mask = target_mask.astype(jnp.float32)[:, None]
    cotangent = (
        upstream.astype(jnp.float32) + weights_mask * head_grad.astype(jnp.float32)
    ).astype(jnp.bfloat16)
    gate_part = jnp.dot(activations, gate_weight, preferred_element_type=jnp.float32)
    up_part = jnp.dot(activations, up_weight, preferred_element_type=jnp.float32)
    hidden_part = transposed(cotangent, down_weight)
    parts = jnp.concatenate([gate_part, up_part, hidden_part], axis=0)
    sums = lax.psum_scatter(parts, "gx", scatter_dimension=1, tiled=True)
    gate_grad, up_grad = swiglu_grads(sums[:rows], sums[rows : 2 * rows], sums[2 * rows :])
    grads = jnp.concatenate([gate_grad, up_grad], axis=0)
    whole = lax.all_gather(grads, "gx", axis=1, tiled=True)
    partial_grad = transposed(whole[:rows], gate_weight) + transposed(whole[rows:], up_weight)
    total_grad = lax.psum(partial_grad, "gy")
    return total_grad.astype(jnp.bfloat16)


def solution(mesh):
    in_specs = (
        P("grp", "gx"),
        P("grp", "gx"),
        P("grp", "gx"),
        P("grp"),
        P("gx", "gy"),
        P("gx", "gy"),
        P("gy", "gx"),
    )
    out_specs = P("grp", "gx")
    return jax.shard_map(shards, mesh=mesh, in_specs=in_specs, out_specs=out_specs, check_vma=False)
```

```python
import functools

import jax
import jax.numpy as jnp
from jax import lax
from jax.experimental import pallas as pl
from jax.experimental.pallas import tpu as pltpu
from jax.sharding import PartitionSpec as P

LANE = 128
NX, NZ = 2, 4
HALF = NZ * LANE
CHUNK = NX * HALF
LAG_B, LAG_C, LAG_D, LAG_E = 2, 3, 4, 5
KEEP = 4


def transposed(left, weight):
    return lax.dot_general(
        left, weight, (((1,), (1,)), ((), ())), preferred_element_type=jnp.float32
    )


def swiglu_grads(gate_proj, up_proj, hidden_grad):
    sigmoid_gate = jax.nn.sigmoid(gate_proj)
    gate_grad = hidden_grad * up_proj * sigmoid_gate * (1.0 + gate_proj * (1.0 - sigmoid_gate))
    up_grad = hidden_grad * gate_proj * sigmoid_gate
    return (gate_grad.astype(jnp.bfloat16), up_grad.astype(jnp.bfloat16))


def plain_shards(activations, upstream, head_grad, target_mask, gate_weight, up_weight, down_weight):
    rows = activations.shape[0]
    weights_mask = target_mask.astype(jnp.float32)[:, None]
    cotangent = (
        upstream.astype(jnp.float32) + weights_mask * head_grad.astype(jnp.float32)
    ).astype(jnp.bfloat16)
    gate_part = jnp.dot(activations, gate_weight, preferred_element_type=jnp.float32)
    up_part = jnp.dot(activations, up_weight, preferred_element_type=jnp.float32)
    hidden_part = transposed(cotangent, down_weight)
    parts = jnp.concatenate([gate_part, up_part, hidden_part], axis=0)
    sums = lax.psum_scatter(parts, "gx", scatter_dimension=1, tiled=True)
    gate_grad, up_grad = swiglu_grads(sums[:rows], sums[rows : 2 * rows], sums[2 * rows :])
    grads = jnp.concatenate([gate_grad, up_grad], axis=0)
    whole = lax.all_gather(grads, "gx", axis=1, tiled=True)
    partial_grad = transposed(whole[:rows], gate_weight) + transposed(whole[rows:], up_weight)
    total_grad = lax.psum(partial_grad, "gy")
    return total_grad.astype(jnp.bfloat16)


def kernel(
    steps, act_ref, ups_ref, head_ref, mask_ref, gate_hbm, up_hbm, down_hbm, out_ref,
    cot, wg, wu, wd, eg, eu, psend, keep, xrecv, zsend, zrecv, grads, acc, other,
    w_sem, e_sem, x_send, x_recv, z_send, z_recv, a_send, a_recv, d_send, d_recv, c_send, c_recv,
):
    rows = act_ref.shape[0]
    grp, gx, gy = lax.axis_index("grp"), lax.axis_index("gx"), lax.axis_index("gy")
    z, x = gx // NX, gx % NX
    x_peer = (grp, z * NX + (1 - x), gy)
    z_peer = [None] + [(grp, ((z + d) % NZ) * NX + x, gy) for d in range(1, NZ)]
    core_peer = (grp, gx, 1 - gy)
    mesh_id = dict(device_id_type=pl.DeviceIdType.MESH)

    def cols(step):
        return pl.ds(pl.multiple_of(step * CHUNK, CHUNK), CHUNK)

    def weights_in(step):
        slot = step % 2
        return (
            pltpu.make_async_copy(gate_hbm.at[:, cols(step)], wg.at[slot], w_sem.at[slot, 0]),
            pltpu.make_async_copy(up_hbm.at[:, cols(step)], wu.at[slot], w_sem.at[slot, 1]),
            pltpu.make_async_copy(down_hbm.at[cols(step), :], wd.at[slot], w_sem.at[slot, 2]),
        )

    def again_in(step):
        slot = step % 2
        return (
            pltpu.make_async_copy(gate_hbm.at[:, cols(step)], eg.at[slot], e_sem.at[slot, 0]),
            pltpu.make_async_copy(up_hbm.at[:, cols(step)], eu.at[slot], e_sem.at[slot, 1]),
        )

    def x_copy(k):
        return pltpu.make_async_remote_copy(
            psend.at[k], xrecv.at[k], x_send.at[k], x_recv.at[k], device_id=x_peer, **mesh_id
        )

    def z_copy(k, d):
        return pltpu.make_async_remote_copy(
            zsend.at[k, (z + d) % NZ], zrecv.at[k, d - 1], z_send.at[k, d - 1], z_recv.at[k, d - 1],
            device_id=z_peer[d], **mesh_id
        )

    def piece(origin):
        return pl.ds(pl.multiple_of(origin * LANE, LANE), LANE)

    def a_copy(k, d, origin):
        ref = grads.at[k, x, :, piece(origin)]
        return pltpu.make_async_remote_copy(
            ref, ref, a_send.at[k, d - 1], a_recv.at[k, d - 1], device_id=z_peer[d], **mesh_id
        )

    def d_copy(k, side):
        ref = grads.at[k, side]
        return pltpu.make_async_remote_copy(
            ref, ref, d_send.at[k], d_recv.at[k], device_id=x_peer, **mesh_id
        )

    for copy in weights_in(0) + again_in(0):
        copy.start()

    barrier = pltpu.get_barrier_semaphore()
    for peer in [x_peer, core_peer] + z_peer[1:]:
        pl.semaphore_signal(barrier, inc=1, device_id=peer, **mesh_id)
    pl.semaphore_wait(barrier, NZ + 1)

    cot[...] = (
        ups_ref[...].astype(jnp.float32) + mask_ref[...] * head_ref[...].astype(jnp.float32)
    ).astype(jnp.bfloat16)
    acc[...] = jnp.zeros_like(acc)

    def stage_a(k):
        for copy in weights_in(k):
            copy.wait()

        @pl.when(k + 1 < steps)
        def _():
            for copy in weights_in(k + 1):
                copy.start()

        slot = k % 2
        for mine in (False, True):
            side = x if mine else 1 - x
            span = pl.ds(pl.multiple_of(side * HALF, HALF), HALF)
            gate = jnp.dot(act_ref[...], wg[slot, :, span], preferred_element_type=jnp.float32)
            up = jnp.dot(act_ref[...], wu[slot, :, span], preferred_element_type=jnp.float32)
            hidden = transposed(cot[...], wd[slot, span, :])
            for i, value in enumerate((gate, up, hidden)):
                at = pl.ds(i * rows, rows)
                if mine:
                    keep[k % KEEP, at, :] = value
                else:
                    psend[k, at, :] = value.astype(jnp.bfloat16)
            if not mine:
                x_copy(k).start()

    def stage_b(k):
        x_copy(k).wait_recv()
        for j in range(NZ):
            at = pl.ds(j * LANE, LANE)
            total = keep[k % KEEP, :, at] + xrecv[k, :, at].astype(jnp.float32)
            keep[k % KEEP, :, at] = total
            zsend[k, j] = total.astype(jnp.bfloat16)
        for d in range(1, NZ):
            z_copy(k, d).start()

    def stage_c(k):
        for d in range(1, NZ):
            z_copy(k, d).wait_recv()
        parts = []
        for i in range(3):
            at = pl.ds(i * rows, rows)
            total = keep[k % KEEP, at, piece(z)]
            for d in range(1, NZ):
                total = total + zrecv[k, d - 1, at, :].astype(jnp.float32)
            parts.append(total)
        gate_grad, up_grad = swiglu_grads(*parts)
        grads[k, x, pl.ds(0, rows), piece(z)] = gate_grad
        grads[k, x, pl.ds(rows, rows), piece(z)] = up_grad
        for d in range(1, NZ):
            a_copy(k, d, z).start()

    def stage_d(k):
        for d in range(1, NZ):
            a_copy(k, d, (z + NZ - d) % NZ).wait_recv()
        d_copy(k, x).start()

    def stage_e(k):
        for copy in again_in(k):
            copy.wait()

        @pl.when(k + 1 < steps)
        def _():
            for copy in again_in(k + 1):
                copy.start()

        d_copy(k, 1 - x).wait_recv()
        slot = k % 2
        total = acc[...]
        for side in range(NX):
            span = pl.ds(side * HALF, HALF)
            total += transposed(grads[k, side, pl.ds(0, rows), :], eg[slot, :, span])
            total += transposed(grads[k, side, pl.ds(rows, rows), :], eu[slot, :, span])
        acc[...] = total

    def body(t, carry):
        for lag, stage in (
            (0, stage_a), (LAG_B, stage_b), (LAG_C, stage_c), (LAG_D, stage_d), (LAG_E, stage_e)
        ):
            @pl.when(jnp.logical_and(t >= lag, t < steps + lag))
            def _():
                stage(t - lag)
        return carry

    lax.fori_loop(0, steps + LAG_E, body, 0)

    core = pltpu.make_async_remote_copy(acc, other, c_send, c_recv, device_id=core_peer, **mesh_id)
    core.start()

    def drain(k, carry):
        x_copy(k).wait_send()
        for d in range(1, NZ):
            z_copy(k, d).wait_send()
            a_copy(k, d, z).wait_send()
        d_copy(k, x).wait_send()
        return carry

    lax.fori_loop(0, steps, drain, 0)
    core.wait()
    out_ref[...] = (acc[...] + other[...]).astype(out_ref.dtype)


def kernel_shards(activations, upstream, head_grad, target_mask, gate_weight, up_weight, down_weight):
    rows, features = activations.shape
    hidden = gate_weight.shape[1]
    steps = hidden // CHUNK
    mask = target_mask.astype(jnp.float32)[:, None]
    vmem = pl.BlockSpec(memory_space=pltpu.VMEM)
    hbm = pl.BlockSpec(memory_space=pl.ANY)
    dma = pltpu.SemaphoreType.DMA
    bf16, f32 = jnp.bfloat16, jnp.float32
    return pl.pallas_call(
        functools.partial(kernel, steps),
        out_shape=jax.ShapeDtypeStruct((rows, features), bf16),
        in_specs=[vmem] * 4 + [hbm] * 3,
        out_specs=vmem,
        scratch_shapes=[
            pltpu.VMEM((rows, features), bf16),
            pltpu.VMEM((2, features, CHUNK), bf16),
            pltpu.VMEM((2, features, CHUNK), bf16),
            pltpu.VMEM((2, CHUNK, features), bf16),
            pltpu.VMEM((2, features, CHUNK), bf16),
            pltpu.VMEM((2, features, CHUNK), bf16),
            pltpu.VMEM((steps, 3 * rows, HALF), bf16),
            pltpu.VMEM((KEEP, 3 * rows, HALF), f32),
            pltpu.VMEM((steps, 3 * rows, HALF), bf16),
            pltpu.VMEM((steps, NZ, 3 * rows, LANE), bf16),
            pltpu.VMEM((steps, NZ - 1, 3 * rows, LANE), bf16),
            pltpu.VMEM((steps, NX, 2 * rows, HALF), bf16),
            pltpu.VMEM((rows, features), f32),
            pltpu.VMEM((rows, features), f32),
            dma((2, 3)),
            dma((2, 2)),
            dma((steps,)),
            dma((steps,)),
            dma((steps, NZ - 1)),
            dma((steps, NZ - 1)),
            dma((steps, NZ - 1)),
            dma((steps, NZ - 1)),
            dma((steps,)),
            dma((steps,)),
            dma,
            dma,
        ],
        compiler_params=pltpu.CompilerParams(
            collective_id=0, has_side_effects=True, vmem_limit_bytes=60 * 2**20
        ),
        cost_estimate=pl.CostEstimate(
            flops=10 * rows * features * hidden,
            bytes_accessed=10 * features * hidden,
            transcendentals=rows * hidden // 8,
        ),
    )(activations, upstream, head_grad, mask, gate_weight, up_weight, down_weight)


def solution(mesh):
    def shards(*arrays):
        rows, features = arrays[0].shape
        hidden = arrays[4].shape[1]
        fits = (
            mesh.shape["gx"] == NX * NZ
            and mesh.shape["gy"] == 2
            and hidden % CHUNK == 0
            and hidden // CHUNK <= 13
            and rows == 128
            and features == 1024
        )
        return (kernel_shards if fits else plain_shards)(*arrays)

    in_specs = (
        P("grp", "gx"),
        P("grp", "gx"),
        P("grp", "gx"),
        P("grp"),
        P("gx", "gy"),
        P("gx", "gy"),
        P("gy", "gx"),
    )
    out_specs = P("grp", "gx")
    return jax.shard_map(shards, mesh=mesh, in_specs=in_specs, out_specs=out_specs, check_vma=False)
```

```python
import functools

import jax
import jax.numpy as jnp
from jax import lax
from jax.experimental import pallas as pl
from jax.experimental.pallas import tpu as pltpu
from jax.sharding import PartitionSpec as P

LANE = 128
NX, NZ = 2, 4
HALF = NZ * LANE
CHUNK = NX * HALF
LAG_B, LAG_C, LAG_F, LAG_D, LAG_E = 1, 2, 3, 4, 5
CYCLE = 5
KEEP = 4


def transposed(left, weight):
    return lax.dot_general(
        left, weight, (((1,), (1,)), ((), ())), preferred_element_type=jnp.float32
    )


def swiglu_grads(gate_proj, up_proj, hidden_grad):
    sigmoid_gate = jax.nn.sigmoid(gate_proj)
    gate_grad = hidden_grad * up_proj * sigmoid_gate * (1.0 + gate_proj * (1.0 - sigmoid_gate))
    up_grad = hidden_grad * gate_proj * sigmoid_gate
    return (gate_grad.astype(jnp.bfloat16), up_grad.astype(jnp.bfloat16))


def plain_shards(activations, upstream, head_grad, target_mask, gate_weight, up_weight, down_weight):
    rows = activations.shape[0]
    weights_mask = target_mask.astype(jnp.float32)[:, None]
    cotangent = (
        upstream.astype(jnp.float32) + weights_mask * head_grad.astype(jnp.float32)
    ).astype(jnp.bfloat16)
    gate_part = jnp.dot(activations, gate_weight, preferred_element_type=jnp.float32)
    up_part = jnp.dot(activations, up_weight, preferred_element_type=jnp.float32)
    hidden_part = transposed(cotangent, down_weight)
    parts = jnp.concatenate([gate_part, up_part, hidden_part], axis=0)
    sums = lax.psum_scatter(parts, "gx", scatter_dimension=1, tiled=True)
    gate_grad, up_grad = swiglu_grads(sums[:rows], sums[rows : 2 * rows], sums[2 * rows :])
    grads = jnp.concatenate([gate_grad, up_grad], axis=0)
    whole = lax.all_gather(grads, "gx", axis=1, tiled=True)
    partial_grad = transposed(whole[:rows], gate_weight) + transposed(whole[rows:], up_weight)
    total_grad = lax.psum(partial_grad, "gy")
    return total_grad.astype(jnp.bfloat16)


def kernel(
    steps, act_ref, ups_ref, head_ref, mask_ref, gate_hbm, up_hbm, down_hbm, out_ref,
    cot, wg, wu, wd, eg, eu, psend, keep, xrecv, zsend, zrecv, grads, acc, other,
    w_sem, e_sem, x_send, x_recv, z_send, z_recv, a_send, a_recv, d_send, d_recv, c_send, c_recv,
):
    rows = act_ref.shape[0]
    grp, gx, gy = lax.axis_index("grp"), lax.axis_index("gx"), lax.axis_index("gy")
    z, x = gx // NX, gx % NX
    x_peer = (grp, z * NX + (1 - x), gy)
    z_peer = [None] + [(grp, ((z + d) % NZ) * NX + x, gy) for d in range(1, NZ)]
    core_peer = (grp, gx, 1 - gy)
    mesh_id = dict(device_id_type=pl.DeviceIdType.MESH)

    def cols(step):
        return pl.ds(pl.multiple_of(step * CHUNK, CHUNK), CHUNK)

    def weights_in(step):
        slot = step % 2
        return (
            pltpu.make_async_copy(gate_hbm.at[:, cols(step)], wg.at[slot], w_sem.at[slot, 0]),
            pltpu.make_async_copy(up_hbm.at[:, cols(step)], wu.at[slot], w_sem.at[slot, 1]),
            pltpu.make_async_copy(down_hbm.at[cols(step), :], wd.at[slot], w_sem.at[slot, 2]),
        )

    def again_in(step):
        slot = step % 2
        return (
            pltpu.make_async_copy(gate_hbm.at[:, cols(step)], eg.at[slot], e_sem.at[slot, 0]),
            pltpu.make_async_copy(up_hbm.at[:, cols(step)], eu.at[slot], e_sem.at[slot, 1]),
        )

    def x_copy(k):
        return pltpu.make_async_remote_copy(
            psend.at[k], xrecv.at[k], x_send.at[k], x_recv.at[k], device_id=x_peer, **mesh_id
        )

    def z_copy(k, d):
        return pltpu.make_async_remote_copy(
            zsend.at[k, (z + d) % NZ], zrecv.at[k, d - 1], z_send.at[k, d - 1], z_recv.at[k, d - 1],
            device_id=z_peer[d], **mesh_id
        )

    def piece(origin):
        return pl.ds(pl.multiple_of(origin * LANE, LANE), LANE)

    side_z, odd = z // 2, z % 2
    inner = side_z + odd == 1
    mate = (grp, (2 * side_z + 1 - odd) * NX + x, gy)
    across = (grp, (2 - side_z) * NX + x, gy)

    def early(k):
        return (k % CYCLE) % 2 == 1

    def both(k, run):
        @pl.when(early(k))
        def _():
            run(True)

        @pl.when(jnp.logical_not(early(k)))
        def _():
            run(False)

    def gathered(k, first, span):
        return grads.at[k, :, :, span] if first else grads.at[k, x, :, span]

    def mate_copy(k, origin, first):
        ref = gathered(k, first, piece(origin))
        return pltpu.make_async_remote_copy(
            ref, ref, a_send.at[k, 0], a_recv.at[k, 0], device_id=mate, **mesh_id
        )

    def across_copy(k, origin, first):
        ref = gathered(k, first, piece(origin))
        return pltpu.make_async_remote_copy(
            ref, ref, a_send.at[k, 1], a_recv.at[k, 1 + origin % 2], device_id=across, **mesh_id
        )

    def pair_copy(k, side, first):
        start = pl.multiple_of(side * 2 * LANE, 2 * LANE)
        ref = gathered(k, first, pl.ds(start, 2 * LANE))
        return pltpu.make_async_remote_copy(
            ref, ref, a_send.at[k, 2], a_recv.at[k, 3], device_id=mate, **mesh_id
        )

    def own_copy(k, side):
        ref = grads.at[k, side, :, piece(z)]
        return pltpu.make_async_remote_copy(
            ref, ref, d_send.at[k], d_recv.at[k], device_id=x_peer, **mesh_id
        )

    def d_copy(k, side):
        ref = grads.at[k, side]
        return pltpu.make_async_remote_copy(
            ref, ref, d_send.at[k], d_recv.at[k], device_id=x_peer, **mesh_id
        )

    for copy in weights_in(0) + again_in(0):
        copy.start()

    barrier = pltpu.get_barrier_semaphore()
    for peer in [x_peer, core_peer] + z_peer[1:]:
        pl.semaphore_signal(barrier, inc=1, device_id=peer, **mesh_id)
    pl.semaphore_wait(barrier, NZ + 1)

    cot[...] = (
        ups_ref[...].astype(jnp.float32) + mask_ref[...] * head_ref[...].astype(jnp.float32)
    ).astype(jnp.bfloat16)
    acc[...] = jnp.zeros_like(acc)

    def stage_a(k):
        for copy in weights_in(k):
            copy.wait()

        @pl.when(k + 1 < steps)
        def _():
            for copy in weights_in(k + 1):
                copy.start()

        slot = k % 2
        for mine in (False, True):
            side = x if mine else 1 - x
            span = pl.ds(pl.multiple_of(side * HALF, HALF), HALF)
            gate = jnp.dot(act_ref[...], wg[slot, :, span], preferred_element_type=jnp.float32)
            up = jnp.dot(act_ref[...], wu[slot, :, span], preferred_element_type=jnp.float32)
            hidden = transposed(cot[...], wd[slot, span, :])
            for i, value in enumerate((gate, up, hidden)):
                at = pl.ds(i * rows, rows)
                if mine:
                    keep[k % KEEP, at, :] = value
                else:
                    psend[k, at, :] = value.astype(jnp.bfloat16)
            if not mine:
                x_copy(k).start()

    def stage_b(k):
        x_copy(k).wait_recv()
        for j in range(NZ):
            at = pl.ds(j * LANE, LANE)
            total = keep[k % KEEP, :, at] + xrecv[k, :, at].astype(jnp.float32)
            keep[k % KEEP, :, at] = total
            zsend[k, j] = total.astype(jnp.bfloat16)
        for d in range(1, NZ):
            z_copy(k, d).start()

    def stage_c(k):
        for d in range(1, NZ):
            z_copy(k, d).wait_recv()
        parts = []
        for i in range(3):
            at = pl.ds(i * rows, rows)
            total = keep[k % KEEP, at, piece(z)]
            for d in range(1, NZ):
                total = total + zrecv[k, d - 1, at, :].astype(jnp.float32)
            parts.append(total)
        gate_grad, up_grad = swiglu_grads(*parts)
        grads[k, x, pl.ds(0, rows), piece(z)] = gate_grad
        grads[k, x, pl.ds(rows, rows), piece(z)] = up_grad

        def send(first):
            if first:
                own_copy(k, x).start()
            else:
                mate_copy(k, z, first).start()
                across_copy(k, z, first).start()

        both(k, send)

    def spread(k):
        own_copy(k, 1 - x).wait_recv()
        mate_copy(k, z, True).start()
        across_copy(k, z, True).start()

    def forward(k, first):
        @pl.when(inner)
        def _():
            for i in range(2):
                across_copy(k, 2 * (1 - side_z) + i, first).wait_recv()
            pair_copy(k, 1 - side_z, first).start()

    def arrived(k, first):
        mate_copy(k, z, first).wait_recv()

        @pl.when(jnp.logical_not(inner))
        def _():
            pair_copy(k, 1 - side_z, first).wait_recv()

    def stage_f(k):
        both(k, lambda first: spread(k) if first else forward(k, False))

    def stage_d(k):
        def run(first):
            if first:
                forward(k, True)
            else:
                arrived(k, False)
                d_copy(k, x).start()

        both(k, run)

    def stage_e(k):
        for copy in again_in(k):
            copy.wait()

        @pl.when(k + 1 < steps)
        def _():
            for copy in again_in(k + 1):
                copy.start()

        both(k, lambda first: arrived(k, True) if first else d_copy(k, 1 - x).wait_recv())
        slot = k % 2
        total = acc[...]
        for side in range(NX):
            span = pl.ds(side * HALF, HALF)
            total += transposed(grads[k, side, pl.ds(0, rows), :], eg[slot, :, span])
            total += transposed(grads[k, side, pl.ds(rows, rows), :], eu[slot, :, span])
        acc[...] = total

    def body(t, carry):
        for lag, stage in (
            (0, stage_a), (LAG_B, stage_b), (LAG_C, stage_c),
            (LAG_F, stage_f), (LAG_D, stage_d), (LAG_E, stage_e),
        ):
            @pl.when(jnp.logical_and(t >= lag, t < steps + lag))
            def _():
                stage(t - lag)
        return carry

    lax.fori_loop(0, steps + LAG_E, body, 0)

    core = pltpu.make_async_remote_copy(acc, other, c_send, c_recv, device_id=core_peer, **mesh_id)
    core.start()

    def drain(k, carry):
        x_copy(k).wait_send()
        for d in range(1, NZ):
            z_copy(k, d).wait_send()

        def sent(first):
            mate_copy(k, z, first).wait_send()
            across_copy(k, z, first).wait_send()

            @pl.when(inner)
            def _():
                pair_copy(k, 1 - side_z, first).wait_send()

            (own_copy if first else d_copy)(k, x).wait_send()

        both(k, sent)
        return carry

    lax.fori_loop(0, steps, drain, 0)
    core.wait()
    out_ref[...] = (acc[...] + other[...]).astype(out_ref.dtype)


def kernel_shards(activations, upstream, head_grad, target_mask, gate_weight, up_weight, down_weight):
    rows, features = activations.shape
    hidden = gate_weight.shape[1]
    steps = hidden // CHUNK
    mask = target_mask.astype(jnp.float32)[:, None]
    vmem = pl.BlockSpec(memory_space=pltpu.VMEM)
    hbm = pl.BlockSpec(memory_space=pl.ANY)
    dma = pltpu.SemaphoreType.DMA
    bf16, f32 = jnp.bfloat16, jnp.float32
    return pl.pallas_call(
        functools.partial(kernel, steps),
        out_shape=jax.ShapeDtypeStruct((rows, features), bf16),
        in_specs=[vmem] * 4 + [hbm] * 3,
        out_specs=vmem,
        scratch_shapes=[
            pltpu.VMEM((rows, features), bf16),
            pltpu.VMEM((2, features, CHUNK), bf16),
            pltpu.VMEM((2, features, CHUNK), bf16),
            pltpu.VMEM((2, CHUNK, features), bf16),
            pltpu.VMEM((2, features, CHUNK), bf16),
            pltpu.VMEM((2, features, CHUNK), bf16),
            pltpu.VMEM((steps, 3 * rows, HALF), bf16),
            pltpu.VMEM((KEEP, 3 * rows, HALF), f32),
            pltpu.VMEM((steps, 3 * rows, HALF), bf16),
            pltpu.VMEM((steps, NZ, 3 * rows, LANE), bf16),
            pltpu.VMEM((steps, NZ - 1, 3 * rows, LANE), bf16),
            pltpu.VMEM((steps, NX, 2 * rows, HALF), bf16),
            pltpu.VMEM((rows, features), f32),
            pltpu.VMEM((rows, features), f32),
            dma((2, 3)),
            dma((2, 2)),
            dma((steps,)),
            dma((steps,)),
            dma((steps, NZ - 1)),
            dma((steps, NZ - 1)),
            dma((steps, 3)),
            dma((steps, 4)),
            dma((steps,)),
            dma((steps,)),
            dma,
            dma,
        ],
        compiler_params=pltpu.CompilerParams(
            collective_id=0, has_side_effects=True, vmem_limit_bytes=60 * 2**20
        ),
        cost_estimate=pl.CostEstimate(
            flops=10 * rows * features * hidden,
            bytes_accessed=10 * features * hidden,
            transcendentals=rows * hidden // 8,
        ),
    )(activations, upstream, head_grad, mask, gate_weight, up_weight, down_weight)


def solution(mesh):
    def shards(*arrays):
        rows, features = arrays[0].shape
        hidden = arrays[4].shape[1]
        fits = (
            mesh.shape["gx"] == NX * NZ
            and mesh.shape["gy"] == 2
            and hidden % CHUNK == 0
            and hidden // CHUNK <= 13
            and rows == 128
            and features == 1024
        )
        return (kernel_shards if fits else plain_shards)(*arrays)

    in_specs = (
        P("grp", "gx"),
        P("grp", "gx"),
        P("grp", "gx"),
        P("grp"),
        P("gx", "gy"),
        P("gx", "gy"),
        P("gy", "gx"),
    )
    out_specs = P("grp", "gx")
    return jax.shard_map(shards, mesh=mesh, in_specs=in_specs, out_specs=out_specs, check_vma=False)
```

```python
import functools

import jax
import jax.numpy as jnp
from jax import lax
from jax.experimental import pallas as pl
from jax.experimental.pallas import tpu as pltpu
from jax.sharding import PartitionSpec as P

LANE = 128
NX, NZ = 2, 4
HALF = NZ * LANE
CHUNK = NX * HALF
LAG_B, LAG_C, LAG_F, LAG_D, LAG_E = 2, 3, 4, 5, 6
CYCLE = 3
KEEP = 4


def transposed(left, weight):
    return lax.dot_general(
        left, weight, (((1,), (1,)), ((), ())), preferred_element_type=jnp.float32
    )


def swiglu_grads(gate_proj, up_proj, hidden_grad):
    sigmoid_gate = jax.nn.sigmoid(gate_proj)
    gate_grad = hidden_grad * up_proj * sigmoid_gate * (1.0 + gate_proj * (1.0 - sigmoid_gate))
    up_grad = hidden_grad * gate_proj * sigmoid_gate
    return (gate_grad.astype(jnp.bfloat16), up_grad.astype(jnp.bfloat16))


def plain_shards(activations, upstream, head_grad, target_mask, gate_weight, up_weight, down_weight):
    rows = activations.shape[0]
    weights_mask = target_mask.astype(jnp.float32)[:, None]
    cotangent = (
        upstream.astype(jnp.float32) + weights_mask * head_grad.astype(jnp.float32)
    ).astype(jnp.bfloat16)
    gate_part = jnp.dot(activations, gate_weight, preferred_element_type=jnp.float32)
    up_part = jnp.dot(activations, up_weight, preferred_element_type=jnp.float32)
    hidden_part = transposed(cotangent, down_weight)
    parts = jnp.concatenate([gate_part, up_part, hidden_part], axis=0)
    sums = lax.psum_scatter(parts, "gx", scatter_dimension=1, tiled=True)
    gate_grad, up_grad = swiglu_grads(sums[:rows], sums[rows : 2 * rows], sums[2 * rows :])
    grads = jnp.concatenate([gate_grad, up_grad], axis=0)
    whole = lax.all_gather(grads, "gx", axis=1, tiled=True)
    partial_grad = transposed(whole[:rows], gate_weight) + transposed(whole[rows:], up_weight)
    total_grad = lax.psum(partial_grad, "gy")
    return total_grad.astype(jnp.bfloat16)


def kernel(
    steps, act_ref, ups_ref, head_ref, mask_ref, gate_hbm, up_hbm, down_hbm, out_ref,
    cot, wg, wu, wd, eg, eu, psend, keep, xrecv, zsend, zrecv, grads, acc, other,
    w_sem, e_sem, x_send, x_recv, z_send, z_recv, a_send, a_recv, d_send, d_recv, c_send, c_recv,
):
    rows = act_ref.shape[0]
    grp, gx, gy = lax.axis_index("grp"), lax.axis_index("gx"), lax.axis_index("gy")
    z, x = gx // NX, gx % NX
    x_peer = (grp, z * NX + (1 - x), gy)
    z_peer = [None] + [(grp, ((z + d) % NZ) * NX + x, gy) for d in range(1, NZ)]
    core_peer = (grp, gx, 1 - gy)
    mesh_id = dict(device_id_type=pl.DeviceIdType.MESH)

    def cols(step):
        return pl.ds(pl.multiple_of(step * CHUNK, CHUNK), CHUNK)

    def weights_in(step):
        slot = step % 2
        return (
            pltpu.make_async_copy(gate_hbm.at[:, cols(step)], wg.at[slot], w_sem.at[slot, 0]),
            pltpu.make_async_copy(up_hbm.at[:, cols(step)], wu.at[slot], w_sem.at[slot, 1]),
            pltpu.make_async_copy(down_hbm.at[cols(step), :], wd.at[slot], w_sem.at[slot, 2]),
        )

    def again_in(step):
        slot = step % 2
        return (
            pltpu.make_async_copy(gate_hbm.at[:, cols(step)], eg.at[slot], e_sem.at[slot, 0]),
            pltpu.make_async_copy(up_hbm.at[:, cols(step)], eu.at[slot], e_sem.at[slot, 1]),
        )

    def x_copy(k):
        return pltpu.make_async_remote_copy(
            psend.at[k], xrecv.at[k], x_send.at[k], x_recv.at[k], device_id=x_peer, **mesh_id
        )

    def z_copy(k, d):
        return pltpu.make_async_remote_copy(
            zsend.at[k, (z + d) % NZ], zrecv.at[k, d - 1], z_send.at[k, d - 1], z_recv.at[k, d - 1],
            device_id=z_peer[d], **mesh_id
        )

    def piece(origin):
        return pl.ds(pl.multiple_of(origin * LANE, LANE), LANE)

    side_z, odd = z // 2, z % 2
    inner = side_z + odd == 1
    mate = (grp, (2 * side_z + 1 - odd) * NX + x, gy)
    across = (grp, (2 - side_z) * NX + x, gy)

    def early(k):
        return k % CYCLE == 0

    def both(k, run):
        @pl.when(early(k))
        def _():
            run(True)

        @pl.when(jnp.logical_not(early(k)))
        def _():
            run(False)

    def gathered(k, first, span):
        return grads.at[k, :, :, span] if first else grads.at[k, x, :, span]

    def mate_copy(k, origin, first):
        ref = gathered(k, first, piece(origin))
        return pltpu.make_async_remote_copy(
            ref, ref, a_send.at[k, 0], a_recv.at[k, 0], device_id=mate, **mesh_id
        )

    def across_copy(k, origin, first):
        ref = gathered(k, first, piece(origin))
        return pltpu.make_async_remote_copy(
            ref, ref, a_send.at[k, 1], a_recv.at[k, 1 + origin % 2], device_id=across, **mesh_id
        )

    def pair_copy(k, side, first):
        start = pl.multiple_of(side * 2 * LANE, 2 * LANE)
        ref = gathered(k, first, pl.ds(start, 2 * LANE))
        return pltpu.make_async_remote_copy(
            ref, ref, a_send.at[k, 2], a_recv.at[k, 3], device_id=mate, **mesh_id
        )

    def own_copy(k, side):
        ref = grads.at[k, side, :, piece(z)]
        return pltpu.make_async_remote_copy(
            ref, ref, d_send.at[k], d_recv.at[k], device_id=x_peer, **mesh_id
        )

    def d_copy(k, side):
        ref = grads.at[k, side]
        return pltpu.make_async_remote_copy(
            ref, ref, d_send.at[k], d_recv.at[k], device_id=x_peer, **mesh_id
        )

    for copy in weights_in(0) + again_in(0):
        copy.start()

    barrier = pltpu.get_barrier_semaphore()
    for peer in [x_peer, core_peer] + z_peer[1:]:
        pl.semaphore_signal(barrier, inc=1, device_id=peer, **mesh_id)
    pl.semaphore_wait(barrier, NZ + 1)

    cot[...] = (
        ups_ref[...].astype(jnp.float32) + mask_ref[...] * head_ref[...].astype(jnp.float32)
    ).astype(jnp.bfloat16)
    acc[...] = jnp.zeros_like(acc)

    def stage_a(k):
        for copy in weights_in(k):
            copy.wait()

        @pl.when(k + 1 < steps)
        def _():
            for copy in weights_in(k + 1):
                copy.start()

        slot = k % 2
        for mine in (False, True):
            side = x if mine else 1 - x
            span = pl.ds(pl.multiple_of(side * HALF, HALF), HALF)
            gate = jnp.dot(act_ref[...], wg[slot, :, span], preferred_element_type=jnp.float32)
            up = jnp.dot(act_ref[...], wu[slot, :, span], preferred_element_type=jnp.float32)
            hidden = transposed(cot[...], wd[slot, span, :])
            for i, value in enumerate((gate, up, hidden)):
                at = pl.ds(i * rows, rows)
                if mine:
                    keep[k % KEEP, at, :] = value
                else:
                    psend[k, at, :] = value.astype(jnp.bfloat16)
            if not mine:
                x_copy(k).start()

    def stage_b(k):
        x_copy(k).wait_recv()
        for j in range(NZ):
            at = pl.ds(j * LANE, LANE)
            total = keep[k % KEEP, :, at] + xrecv[k, :, at].astype(jnp.float32)
            keep[k % KEEP, :, at] = total
            zsend[k, j] = total.astype(jnp.bfloat16)
        for d in range(1, NZ):
            z_copy(k, d).start()

    def stage_c(k):
        for d in range(1, NZ):
            z_copy(k, d).wait_recv()
        parts = []
        for i in range(3):
            at = pl.ds(i * rows, rows)
            total = keep[k % KEEP, at, piece(z)]
            for d in range(1, NZ):
                total = total + zrecv[k, d - 1, at, :].astype(jnp.float32)
            parts.append(total)
        gate_grad, up_grad = swiglu_grads(*parts)
        grads[k, x, pl.ds(0, rows), piece(z)] = gate_grad
        grads[k, x, pl.ds(rows, rows), piece(z)] = up_grad

        def send(first):
            if first:
                own_copy(k, x).start()
            else:
                mate_copy(k, z, first).start()
                across_copy(k, z, first).start()

        both(k, send)

    def spread(k):
        own_copy(k, 1 - x).wait_recv()
        mate_copy(k, z, True).start()
        across_copy(k, z, True).start()

    def forward(k, first):
        @pl.when(inner)
        def _():
            for i in range(2):
                across_copy(k, 2 * (1 - side_z) + i, first).wait_recv()
            pair_copy(k, 1 - side_z, first).start()

    def arrived(k, first):
        mate_copy(k, z, first).wait_recv()

        @pl.when(jnp.logical_not(inner))
        def _():
            pair_copy(k, 1 - side_z, first).wait_recv()

    def stage_f(k):
        both(k, lambda first: spread(k) if first else forward(k, False))

    def stage_d(k):
        def run(first):
            if first:
                forward(k, True)
            else:
                arrived(k, False)
                d_copy(k, x).start()

        both(k, run)

    def stage_e(k):
        for copy in again_in(k):
            copy.wait()

        @pl.when(k + 1 < steps)
        def _():
            for copy in again_in(k + 1):
                copy.start()

        both(k, lambda first: arrived(k, True) if first else d_copy(k, 1 - x).wait_recv())
        slot = k % 2
        total = acc[...]
        for side in range(NX):
            span = pl.ds(side * HALF, HALF)
            total += transposed(grads[k, side, pl.ds(0, rows), :], eg[slot, :, span])
            total += transposed(grads[k, side, pl.ds(rows, rows), :], eu[slot, :, span])
        acc[...] = total

    def body(t, carry):
        for lag, stage in (
            (0, stage_a), (LAG_B, stage_b), (LAG_C, stage_c),
            (LAG_F, stage_f), (LAG_D, stage_d), (LAG_E, stage_e),
        ):
            @pl.when(jnp.logical_and(t >= lag, t < steps + lag))
            def _():
                stage(t - lag)
        return carry

    lax.fori_loop(0, steps + LAG_E, body, 0)

    core = pltpu.make_async_remote_copy(acc, other, c_send, c_recv, device_id=core_peer, **mesh_id)
    core.start()

    def drain(k, carry):
        x_copy(k).wait_send()
        for d in range(1, NZ):
            z_copy(k, d).wait_send()

        def sent(first):
            mate_copy(k, z, first).wait_send()
            across_copy(k, z, first).wait_send()

            @pl.when(inner)
            def _():
                pair_copy(k, 1 - side_z, first).wait_send()

            (own_copy if first else d_copy)(k, x).wait_send()

        both(k, sent)
        return carry

    lax.fori_loop(0, steps, drain, 0)
    core.wait()
    out_ref[...] = (acc[...] + other[...]).astype(out_ref.dtype)


def kernel_shards(activations, upstream, head_grad, target_mask, gate_weight, up_weight, down_weight):
    rows, features = activations.shape
    hidden = gate_weight.shape[1]
    steps = hidden // CHUNK
    mask = target_mask.astype(jnp.float32)[:, None]
    vmem = pl.BlockSpec(memory_space=pltpu.VMEM)
    hbm = pl.BlockSpec(memory_space=pl.ANY)
    dma = pltpu.SemaphoreType.DMA
    bf16, f32 = jnp.bfloat16, jnp.float32
    return pl.pallas_call(
        functools.partial(kernel, steps),
        out_shape=jax.ShapeDtypeStruct((rows, features), bf16),
        in_specs=[vmem] * 4 + [hbm] * 3,
        out_specs=vmem,
        scratch_shapes=[
            pltpu.VMEM((rows, features), bf16),
            pltpu.VMEM((2, features, CHUNK), bf16),
            pltpu.VMEM((2, features, CHUNK), bf16),
            pltpu.VMEM((2, CHUNK, features), bf16),
            pltpu.VMEM((2, features, CHUNK), bf16),
            pltpu.VMEM((2, features, CHUNK), bf16),
            pltpu.VMEM((steps, 3 * rows, HALF), bf16),
            pltpu.VMEM((KEEP, 3 * rows, HALF), f32),
            pltpu.VMEM((steps, 3 * rows, HALF), bf16),
            pltpu.VMEM((steps, NZ, 3 * rows, LANE), bf16),
            pltpu.VMEM((steps, NZ - 1, 3 * rows, LANE), bf16),
            pltpu.VMEM((steps, NX, 2 * rows, HALF), bf16),
            pltpu.VMEM((rows, features), f32),
            pltpu.VMEM((rows, features), f32),
            dma((2, 3)),
            dma((2, 2)),
            dma((steps,)),
            dma((steps,)),
            dma((steps, NZ - 1)),
            dma((steps, NZ - 1)),
            dma((steps, 3)),
            dma((steps, 4)),
            dma((steps,)),
            dma((steps,)),
            dma,
            dma,
        ],
        compiler_params=pltpu.CompilerParams(
            collective_id=0, has_side_effects=True, vmem_limit_bytes=60 * 2**20
        ),
        cost_estimate=pl.CostEstimate(
            flops=10 * rows * features * hidden,
            bytes_accessed=10 * features * hidden,
            transcendentals=rows * hidden // 8,
        ),
    )(activations, upstream, head_grad, mask, gate_weight, up_weight, down_weight)


def solution(mesh):
    def shards(*arrays):
        rows, features = arrays[0].shape
        hidden = arrays[4].shape[1]
        fits = (
            mesh.shape["gx"] == NX * NZ
            and mesh.shape["gy"] == 2
            and hidden % CHUNK == 0
            and hidden // CHUNK <= 13
            and rows == 128
            and features == 1024
        )
        return (kernel_shards if fits else plain_shards)(*arrays)

    in_specs = (
        P("grp", "gx"),
        P("grp", "gx"),
        P("grp", "gx"),
        P("grp"),
        P("gx", "gy"),
        P("gx", "gy"),
        P("gy", "gx"),
    )
    out_specs = P("grp", "gx")
    return jax.shard_map(shards, mesh=mesh, in_specs=in_specs, out_specs=out_specs, check_vma=False)
```
